32 devices in a mesh: groups: 2 (over y), slab: 4 (over z), pair: 4 (over x, core).
Axes of the slice: x: 2, y: 2, z: 4, core: 2. Of those that a mesh axis runs over, the one named last changes fastest.
Arguments:
- occupancy: float32 [8, 128, 256, 128], P(('groups', 'pair'), 'slab'), parts along dimension 0, may hold values from 0 to 1
- classes: int32 [8, 128, 256, 128], P(('groups', 'pair'), 'slab'), parts along dimension 0, may hold values from 0 to 7
- conductance: float32 [8], replicated, may hold values from 0.1 to 1
- damping: float32 [8], P('groups'), parts along dimension 0, may hold values from 1 to 8
- matches: int32 [8], P('groups'), parts along dimension 0, may hold values from 0 to 3, each once
Outputs:
- correlation: float32 [8, 128, 256, 128], P(('groups', 'pair'), 'slab'), parts along dimension 0
The draws below stay inside these ranges and needn't reach their ends.
There are 2 independent parts, one for each index of `groups`. The reference program is written for one: setup_inputs(seed, part) draws one part's arguments, and reference() takes and returns one part's arrays. A program takes and returns all parts, laid end to end along the dimension named above; an argument that names none is the same for every part. Nothing has to cross between parts.
Inputs may be any that keep to these rules, and one draw needn't show every extreme that they name: A permutation of the 4 submaps; submap s is registered against submap matches[s]. `classes`: a row of the conductance table.
All inputs are finite; a program needn't handle non-finite values.
Results may differ from the reference program's by a relative error of at most 0.0003.
Values sent between devices are 32-bit elements; how exact they have to be, the bound alone decides.
A program may use at most 128 MiB of HBM per device.

```python
import math
import jax
import jax.numpy as jnp
from jax import lax

X = 256
Y = 128
Z = 128
STEPS = 4
NCLASS = 8
SUBMAPS = 4


def touch_ends(entries, key, smallest, largest):
    place = [jax.random.randint(jax.random.fold_in(key, axis), (), 0, length) for axis, length in enumerate(entries.shape)]
    widest = entries.shape.index(max(entries.shape))
    next_to = place[:widest] + [(place[widest] + 1) % entries.shape[widest]] + place[widest + 1:]
    return entries.at[tuple(place)].set(smallest).at[tuple(next_to)].set(largest)


def shard_levels(stream_key, extent, pieces, smallest, largest):
    def one(dim, shards_of):
        draws = jax.random.uniform(jax.random.fold_in(jax.random.fold_in(stream_key, 6), dim), (shards_of,), jnp.float32, smallest / len(pieces), largest / len(pieces))
        return jnp.repeat(jnp.exp(draws), extent[dim] // shards_of).reshape((-1,) + (1,) * (len(extent) - dim - 1))

    loudness = one(*pieces[0])
    for cut in pieces[1:]:
        loudness = loudness * one(*cut)
    return loudness


def setup_inputs(seed: int = 0, part: int = 0) -> dict:
    splits = jax.random.split(jax.random.key(seed), 6)
    own_keys = jax.random.split(jax.random.fold_in(splits[5], part), 6)
    occupancy = jnp.clip(1.0 * jax.random.uniform(own_keys[0], (SUBMAPS, Z, X, Y), jnp.float32) ** shard_levels(own_keys[0], (SUBMAPS, Z, X, Y), ((0, 4), (1, 4)), -0.2, 0.2), 0.0, 1.0)
    classes = touch_ends(jax.random.randint(own_keys[1], (SUBMAPS, Z, X, Y), 0, NCLASS), jax.random.fold_in(own_keys[1], 1), 0, NCLASS - 1).astype(jnp.int32)
    conductance = jnp.clip(jnp.exp(jax.random.uniform(splits[2], (NCLASS,), jnp.float32, math.log(0.1), math.log(1.0))), 0.1, 1.0)
    damping = jnp.clip(jnp.exp(jax.random.uniform(own_keys[3], (SUBMAPS,), jnp.float32, math.log(1.0), math.log(8.0))), 1.0, 8.0)
    matches = jax.random.permutation(own_keys[4], SUBMAPS).astype(jnp.int32)
    return {"occupancy": occupancy, "classes": classes, "conductance": conductance, "damping": damping, "matches": matches}


STEP_SIZE = 1.0 / 6.0
FLOOR_VALUE = 0.01

def neighbours(padded):
    return [padded[2:, 1:-1, 1:-1], padded[:-2, 1:-1, 1:-1], padded[1:-1, 2:, 1:-1], padded[1:-1, :-2, 1:-1], padded[1:-1, 1:-1, 2:], padded[1:-1, 1:-1, :-2]]

def diffuse(volume, conduct):
    outer_rims = neighbours(jnp.pad(conduct, 1))
    for sweep_index in range(STEPS):
        beside_all = neighbours(jnp.pad(volume, 1))
        change = jnp.zeros_like(volume)
        for other_field, other_conduct in zip(beside_all, outer_rims):
            change = change + 0.5 * (conduct + other_conduct) * (other_field - volume)
        volume = volume + STEP_SIZE * change
    return volume

def frequency(length):
    counter = jnp.arange(length, dtype=jnp.int32)
    return (jnp.where(counter < length // 2, counter, counter - length) / length).astype(jnp.float32)

def reference(occupancy, classes, conductance, damping, matches):

    def spectrum(inputs):
        volume, labels = inputs
        smooth = diffuse(volume, conductance[labels])
        transformed = jnp.fft.fftn(smooth, norm='ortho')
        return (jnp.real(transformed), jnp.imag(transformed))
    real_part, imag_part = lax.map(spectrum, (occupancy, classes))
    radius = frequency(Z)[:, None, None] ** 2 + frequency(X)[None, :, None] ** 2 + frequency(Y)[None, None, :] ** 2

    def correlate(position):
        partner = matches[position]
        own_real = real_part[position]
        own_imag = imag_part[position]
        far_real = real_part[partner]
        far_imag = imag_part[partner]
        cross_real = own_real * far_real + own_imag * far_imag
        cross_imag = own_imag * far_real - own_real * far_imag
        magnitude = jnp.sqrt((own_real ** 2 + own_imag ** 2) * (far_real ** 2 + far_imag ** 2) + FLOOR_VALUE ** 2)
        weight = jnp.exp(-damping[position] * radius) / magnitude
        inverse = jnp.fft.ifftn(lax.complex(cross_real * weight, cross_imag * weight), norm='ortho')
        return jnp.real(inverse).astype(jnp.float32)
    return lax.map(correlate, jnp.arange(SUBMAPS, dtype=jnp.int32))
```

```python
import functools
import math

import jax
import jax.numpy as jnp
import ml_dtypes
import numpy as np
from jax import lax
from jax.experimental import pallas as pl
from jax.experimental.pallas import tpu as pltpu
from jax.sharding import PartitionSpec as P

STEPS = 4
STEP_SIZE = 1.0 / 6.0
FLOOR_VALUE = 0.01
PAD = 8
LIMIT = 58 * 1024 * 1024
MESH = pl.DeviceIdType.MESH


FORMS = {1: "bjxy,jk->bkxy", 2: "bzjy,jk->bzky", 3: "bzxj,jk->bzxk"}


def with_halo(shard, sides, width):
    for axis, dim in sides:
        size, length = (lax.axis_size(axis), shard.shape[dim])
        up = [(i, (i + 1) % size) for i in range(size - 1)]
        down = [(j, i) for i, j in up]
        last = lax.slice_in_dim(shard, length - width, length, axis=dim)
        leading = lax.slice_in_dim(shard, 0, width, axis=dim)
        before = lax.ppermute(last, axis, up)
        after = lax.ppermute(leading, axis, down)
        shard = jnp.concatenate([before, shard, after], axis=dim)
    return shard


def tables(length):
    counter = jnp.arange(length, dtype=jnp.int32)
    product = counter[:, None] * counter[None, :] % length
    angles = product.astype(jnp.float32) * (2.0 * math.pi / length)
    factor = 1.0 / math.sqrt(length)
    return (jnp.cos(angles) * factor, jnp.sin(angles) * factor)


def multiply_along(values, matrix, axis_dim):
    return jnp.einsum(FORMS[axis_dim], values, matrix, precision=lax.Precision.HIGHEST)


def forward_real(values, axis_dim):
    cosine, sine_table = tables(values.shape[axis_dim])
    return (multiply_along(values, cosine, axis_dim), -multiply_along(values, sine_table, axis_dim))


def forward_complex(real_part, imag_part, axis_dim):
    cosine, sine_table = tables(real_part.shape[axis_dim])
    return (
        multiply_along(real_part, cosine, axis_dim)
        + multiply_along(imag_part, sine_table, axis_dim),
        multiply_along(imag_part, cosine, axis_dim)
        - multiply_along(real_part, sine_table, axis_dim),
    )


def inverse_complex(real_part, imag_part, axis_dim):
    cosine, sine_table = tables(real_part.shape[axis_dim])
    return (
        multiply_along(real_part, cosine, axis_dim)
        - multiply_along(imag_part, sine_table, axis_dim),
        multiply_along(imag_part, cosine, axis_dim)
        + multiply_along(real_part, sine_table, axis_dim),
    )


def inverse_real(real_part, imag_part, axis_dim):
    cosine, sine_table = tables(real_part.shape[axis_dim])
    return multiply_along(real_part, cosine, axis_dim) - multiply_along(
        imag_part, sine_table, axis_dim
    )


def local_neighbours(padded):
    widened = jnp.pad(padded, ((0, 0), (0, 0), (1, 1), (1, 1)))
    return [
        widened[:, 2:, 1:-1, 1:-1],
        widened[:, :-2, 1:-1, 1:-1],
        widened[:, 1:-1, 2:, 1:-1],
        widened[:, 1:-1, :-2, 1:-1],
        widened[:, 1:-1, 1:-1, 2:],
        widened[:, 1:-1, 1:-1, :-2],
    ]


def signed_frequency(counter, length):
    return jnp.where(counter < length // 2, counter, counter - length).astype(jnp.float32) / length


def cross_power(own_real, own_imag, far_real, far_imag, decay_rate, offset, whole_rows):
    depth_count = own_real.shape[1]
    row_count = own_real.shape[2]
    width_count = own_real.shape[3]
    along_depth = signed_frequency(jnp.arange(depth_count, dtype=jnp.int32), depth_count)
    along_rows = signed_frequency(offset + jnp.arange(row_count, dtype=jnp.int32), whole_rows)
    along_width = signed_frequency(jnp.arange(width_count, dtype=jnp.int32), width_count)
    radius = (
        along_depth[:, None, None] ** 2
        + along_rows[None, :, None] ** 2
        + along_width[None, None, :] ** 2
    )
    cross_real = own_real * far_real + own_imag * far_imag
    cross_imag = own_imag * far_real - own_real * far_imag
    magnitude = jnp.sqrt((own_real**2 + own_imag**2) * (far_real**2 + far_imag**2) + FLOOR_VALUE**2)
    weight = jnp.exp(-decay_rate[:, None, None, None] * radius[None]) / magnitude
    return (cross_real * weight, cross_imag * weight)


def picked(values, matches):
    return jnp.stack(
        [
            lax.dynamic_index_in_dim(values, matches[i], 0, keepdims=False)
            for i in range(matches.shape[0])
        ]
    )


def spread(values):
    values = lax.all_to_all(values, "pair", split_axis=2, concat_axis=0, tiled=True)
    return lax.all_to_all(values, "slab", split_axis=2, concat_axis=1, tiled=True)


def gathered(values):
    values = lax.all_to_all(values, "slab", split_axis=1, concat_axis=2, tiled=True)
    return lax.all_to_all(values, "pair", split_axis=0, concat_axis=2, tiled=True)


def plain(occupancy, classes, conductance, damping, matches):
    conduct = jnp.zeros(occupancy.shape, jnp.float32)
    for class_id in range(conductance.shape[0]):
        conduct = jnp.where(classes == class_id, conductance[class_id], conduct)
    outer_rims = local_neighbours(with_halo(conduct, (("slab", 1),), 1))
    volume = occupancy
    for sweep_index in range(STEPS):
        beside_all = local_neighbours(with_halo(volume, (("slab", 1),), 1))
        change = jnp.zeros_like(volume)
        for other_field, other_conduct in zip(beside_all, outer_rims):
            change = change + 0.5 * (conduct + other_conduct) * (other_field - volume)
        volume = volume + STEP_SIZE * change
    whole_rows = volume.shape[2]
    real_part, imag_part = forward_real(volume, 3)
    real_part, imag_part = forward_complex(real_part, imag_part, 2)
    real_part, imag_part = (spread(real_part), spread(imag_part))
    real_part, imag_part = forward_complex(real_part, imag_part, 1)
    far_real = picked(real_part, matches)
    far_imag = picked(imag_part, matches)
    offset = (
        lax.axis_index("pair") * lax.axis_size("slab") + lax.axis_index("slab")
    ) * real_part.shape[2]
    cross_real, cross_imag = cross_power(
        real_part, imag_part, far_real, far_imag, damping, offset, whole_rows
    )
    cross_real, cross_imag = inverse_complex(cross_real, cross_imag, 1)
    back_real, back_imag = (gathered(cross_real), gathered(cross_imag))
    back_real, back_imag = inverse_complex(back_real, back_imag, 2)
    return inverse_real(back_real, back_imag, 3)


def halves(matrix):
    high = matrix.astype(np.float32).astype(ml_dtypes.bfloat16)
    low = (matrix - high.astype(np.float64)).astype(ml_dtypes.bfloat16)
    return high, low


def trig(rows, cols, length):
    angle = 2.0 * np.pi * ((np.asarray(rows)[:, None] * np.asarray(cols)[None, :]) % length) / length
    return np.cos(angle) / math.sqrt(length), np.sin(angle) / math.sqrt(length)


def swapped(matrix, axis):
    first, second = np.split(matrix, 2, axis)
    return np.concatenate([second, -first], axis)


def row_order(length, blocks):
    half = length // blocks // 2
    order = []
    for block in range(blocks):
        ahead = [block * half + j for j in range(half)]
        order += ahead + [(length - k) if k else length // 2 for k in ahead]
    return np.array(order)


def forward_y(length):
    half = length // 2
    cosine, sine = trig(np.arange(length), np.arange(half), length)
    imag = -sine
    imag[:, 0] = (1.0 - 2.0 * (np.arange(length) % 2)) / math.sqrt(length)
    table = np.concatenate([cosine, imag], 1)
    return np.concatenate([table, swapped(table, 1)], 1)


def inverse_y(length):
    half = length // 2
    cosine, sine = trig(np.arange(half), np.arange(length), length)
    real, imag = 2.0 * cosine, -2.0 * sine
    real[0] = 1.0 / math.sqrt(length)
    imag[0] = (1.0 - 2.0 * (np.arange(length) % 2)) / math.sqrt(length)
    table = np.concatenate([real, imag], 0)
    other = np.concatenate([-imag, real], 0)
    return np.concatenate([table, other], 1)


def forward_x(length, blocks):
    cosine, sine = trig(row_order(length, blocks), np.arange(length), length)
    return np.concatenate([cosine, sine], 1)


def inverse_x(length, blocks):
    cosine, sine = trig(np.arange(length), row_order(length, blocks), length)
    return np.concatenate([cosine, -sine], 1)


def both_z(length):
    cosine, sine = trig(np.arange(length), np.arange(length), length)
    return np.concatenate([cosine, sine], 1), np.concatenate([cosine, -sine], 1)


def squared(length):
    counter = np.arange(length)
    return (np.where(counter < length // 2, counter, counter - length) / length) ** 2


def radii(depth, width):
    half = width // 2
    lanes = np.arange(width) % half
    along = squared(width)[lanes]
    first = squared(depth)[:, None] + along[None, :]
    other = along.copy()
    other[lanes == 0] = 0.25
    second = squared(depth)[:, None] + other[None, :]
    corner = np.zeros(width)
    corner[lanes == 1], corner[lanes == 2], corner[lanes == 3] = 0.25, 0.25, 0.5
    third = squared(depth)[:, None] + corner[None, :]
    return np.stack([first, second, third]).astype(np.float32)


def split(values):
    high = values.astype(jnp.bfloat16)
    return high, (values - high.astype(jnp.float32)).astype(jnp.bfloat16)


def dot(a, b):
    return jnp.dot(a, b, preferred_element_type=jnp.float32)


def left(matrix, values):
    high, low = split(values)
    return dot(matrix[0][...], high) + (dot(matrix[0][...], low) + dot(matrix[1][...], high))


def right(values, matrix):
    high, low = split(values)
    return dot(high, matrix[0][...]) + (dot(low, matrix[0][...]) + dot(high, matrix[1][...]))


def planes_transformed(first, second, along_y, along_x):
    rows, lanes = first.shape
    mid = right(jnp.concatenate([first, second], 0), along_y)
    mid = jnp.concatenate(
        [
            jnp.concatenate([mid[:rows, :lanes], mid[rows:, :lanes]], 1),
            jnp.concatenate([mid[:rows, lanes:], mid[rows:, lanes:]], 1),
        ],
        0,
    )
    out = left(along_x, mid)
    return out[:, :lanes], out[:, lanes:]


def diffuse_kernel(
    slabs, cond, occ, cls, yh, yl, xh, xl, out, buf_a, buf_b, cx, cy, cz, kept, halo, ends, send, recv
):
    depth, rows, lanes = occ.shape
    tile = min(64, rows)
    me = lax.axis_index("slab")
    has_low, has_high = me > 0, me < slabs - 1
    low, high = lax.max(me - 1, 0), lax.min(me + 1, slabs - 1)

    barrier = pltpu.get_barrier_semaphore()

    @pl.when(has_low)
    def _():
        pl.semaphore_signal(barrier, inc=1, device_id={"slab": low}, device_id_type=MESH)

    @pl.when(has_high)
    def _():
        pl.semaphore_signal(barrier, inc=1, device_id={"slab": high}, device_id_type=MESH)

    inside = pl.ds(PAD, rows)

    def conduct(plane):
        labels = cls[plane]
        value = jnp.full((rows, lanes), cond[0], jnp.float32)
        for k in range(1, cond.shape[0]):
            value = jnp.where(labels == k, cond[k], value)
        return value

    ends[0] = conduct(0)
    ends[1] = conduct(depth - 1)

    pl.semaphore_wait(barrier, lax.min(me, 1) + lax.min(slabs - 1 - me, 1))

    def copies(slot, lowest, highest):
        down = pltpu.make_async_remote_copy(
            lowest, halo.at[slot, 1], send.at[slot, 0], recv.at[slot, 1],
            device_id={"slab": low}, device_id_type=MESH,
        )
        up = pltpu.make_async_remote_copy(
            highest, halo.at[slot, 0], send.at[slot, 1], recv.at[slot, 0],
            device_id={"slab": high}, device_id_type=MESH,
        )
        return down, up

    def begin(pair):
        pl.when(has_low)(lambda: pair[0].start())
        pl.when(has_high)(lambda: pair[1].start())

    def arrived(pair):
        pl.when(has_low)(lambda: pair[1].wait_recv())
        pl.when(has_high)(lambda: pair[0].wait_recv())

    def sent(pair):
        pl.when(has_low)(lambda: pair[0].wait_send())
        pl.when(has_high)(lambda: pair[1].wait_send())

    kappas = copies(STEPS, ends.at[0], ends.at[1])
    begin(kappas)
    fields = copies(0, occ.at[0], occ.at[depth - 1])
    begin(fields)

    for slot in range(STEPS + 1):

        @pl.when(jnp.logical_not(has_low))
        def _():
            halo[slot, 0] = jnp.zeros((rows, lanes), jnp.float32)

        @pl.when(jnp.logical_not(has_high))
        def _():
            halo[slot, 1] = jnp.zeros((rows, lanes), jnp.float32)

    edge = jnp.zeros((PAD, lanes), jnp.float32)

    @pl.loop(0, depth)
    def _(z):
        buf_b[z, inside] = conduct(z)
        buf_a[z, inside] = occ[z]
        for ref in (buf_a, buf_b):
            ref[z, pl.ds(0, PAD)] = edge
            ref[z, pl.ds(PAD + rows, PAD)] = edge

    scale = 0.5 * STEP_SIZE

    @pl.loop(0, depth)
    def _(z):
        cx[z, pl.ds(0, PAD)] = scale * (buf_b[z, pl.ds(0, PAD)] + buf_b[z, pl.ds(1, PAD)])
        for r in range(0, rows, tile):
            here = buf_b[z, pl.ds(PAD + r, tile)]
            x_next = buf_b[z, pl.ds(PAD + r + 1, tile)]
            cx[z, pl.ds(PAD + r, tile)] = scale * (here + x_next)
            lane = lax.broadcasted_iota(jnp.int32, (tile, lanes), 1)
            y_next = pltpu.roll(here, lanes - 1, 1)
            cy[z, pl.ds(r, tile)] = jnp.where(lane == lanes - 1, 0.0, scale * (here + y_next))
            rim = (lane == 0) | (lane == lanes - 1)
            kept[z, pl.ds(r, tile)] = 1.0 - jnp.where(rim, scale * here, 0.0)

    @pl.loop(0, depth - 1)
    def _(z):
        cz[z + 1] = scale * (buf_b[z, inside] + buf_b[z + 1, inside])

    arrived(kappas)
    cz[0] = scale * (buf_b[0, inside] + halo[STEPS, 0])
    cz[depth] = scale * (buf_b[depth - 1, inside] + halo[STEPS, 1])

    def update(src, dst, z, r, here, flux_low, flux_high):
        x_next = src[z, pl.ds(PAD + r + 1, tile)]
        x_last = src[z, pl.ds(PAD + r - 1, tile)]
        along_x = cx[z, pl.ds(PAD + r, tile)] * (x_next - here) - cx[
            z, pl.ds(PAD + r - 1, tile)
        ] * (here - x_last)
        flux = cy[z, pl.ds(r, tile)] * (pltpu.roll(here, lanes - 1, 1) - here)
        along_y = flux - pltpu.roll(flux, 1, 1)
        dst[z, pl.ds(PAD + r, tile)] = kept[z, pl.ds(r, tile)] * here + (
            along_x + along_y + (flux_high - flux_low)
        )

    bufs = (buf_a, buf_b)
    for step in range(STEPS):
        src, dst = bufs[step % 2], bufs[1 - step % 2]
        arrived(fields)
        sent(fields)
        for r in range(0, rows, tile):
            at, within = pl.ds(PAD + r, tile), pl.ds(r, tile)
            here, after = src[0, at], src[1, at]
            update(
                src, dst, 0, r, here,
                cz[0, within] * (here - halo[step, 0, within]),
                cz[1, within] * (after - here),
            )
            here, before = src[depth - 1, at], src[depth - 2, at]
            update(
                src, dst, depth - 1, r, here,
                cz[depth - 1, within] * (here - before),
                cz[depth, within] * (halo[step, 1, within] - here),
            )
        if step + 1 < STEPS:
            fields = copies(
                step + 1, dst.at[0, inside], dst.at[depth - 1, inside]
            )
            begin(fields)
        for r in range(0, rows, tile):
            at, within = pl.ds(PAD + r, tile), pl.ds(r, tile)

            def body(z, carry):
                here, flux_low = carry
                after = src[z + 1, at]
                flux_high = cz[z + 1, within] * (after - here)
                update(src, dst, z, r, here, flux_low, flux_high)
                return after, flux_high

            first = src[1, at]
            lax.fori_loop(1, depth - 1, body, (first, cz[1, within] * (first - src[0, at])))
    sent(kappas)

    field = bufs[STEPS % 2]

    @pl.loop(0, depth // 2)
    def _(i):
        one, two = planes_transformed(
            field[2 * i, inside], field[2 * i + 1, inside], (yh, yl), (xh, xl)
        )
        out[2 * i] = one
        out[2 * i + 1] = two


def diffused(occupancy, classes, conductance, slabs, pairs):
    depth, rows, lanes = occupancy.shape
    vmem = pl.BlockSpec(memory_space=pltpu.VMEM)
    y = halves(forward_y(lanes))
    x = halves(forward_x(rows, slabs * pairs))
    padded = (depth, rows + 2 * PAD, lanes)
    return pl.pallas_call(
        functools.partial(diffuse_kernel, slabs),
        out_shape=jax.ShapeDtypeStruct((depth, rows, lanes), jnp.float32),
        in_specs=[pl.BlockSpec(memory_space=pltpu.SMEM)] + [vmem] * 6,
        out_specs=vmem,
        scratch_shapes=[
            pltpu.VMEM(padded, jnp.float32),
            pltpu.VMEM(padded, jnp.float32),
            pltpu.VMEM((depth, rows + PAD, lanes), jnp.float32),
            pltpu.VMEM((depth, rows, lanes), jnp.float32),
            pltpu.VMEM((depth + 1, rows, lanes), jnp.float32),
            pltpu.VMEM((depth, rows, lanes), jnp.float32),
            pltpu.VMEM((STEPS + 1, 2, rows, lanes), jnp.float32),
            pltpu.VMEM((2, rows, lanes), jnp.float32),
            pltpu.SemaphoreType.DMA((STEPS + 1, 2)),
            pltpu.SemaphoreType.DMA((STEPS + 1, 2)),
        ],
        compiler_params=pltpu.CompilerParams(
            collective_id=0, has_side_effects=True, vmem_limit_bytes=LIMIT
        ),
        name="diffuse",
    )(conductance, occupancy, classes, *y, *x)


def exchange_kernel(slabs, pairs, pick, src, dst, own_sem, send, recv):
    slab, pair = lax.axis_index("slab"), lax.axis_index("pair")
    shifts = [
        (dp, dq)
        for dq in sorted(range(slabs), key=lambda q: -min(q, slabs - q))
        for dp in range(pairs)
        if (dp, dq) != (0, 0)
    ]
    barrier = pltpu.get_barrier_semaphore()
    peers = [(lax.rem(pair + dp, pairs), lax.rem(slab + dq, slabs)) for dp, dq in shifts]
    for p, q in peers:
        pl.semaphore_signal(barrier, inc=1, device_id={"pair": p, "slab": q}, device_id_type=MESH)
    pl.semaphore_wait(barrier, len(peers))
    copies = []
    for i, (p, q) in enumerate(peers):
        source, target = pick(src, dst, pair, slab, p, q)
        copy = pltpu.make_async_remote_copy(
            source, target, send.at[i], recv.at[i],
            device_id={"pair": p, "slab": q}, device_id_type=MESH,
        )
        copy.start()
        copies.append(copy)
    source, target = pick(src, dst, pair, slab, pair, slab)
    own = pltpu.make_async_copy(source, target, own_sem)
    own.start()
    own.wait()
    for copy in copies:
        copy.wait_recv()
    for copy in copies:
        copy.wait_send()


def exchange(values, shape, pick, slabs, pairs, collective_id, name):
    anywhere = pl.BlockSpec(memory_space=pl.ANY)
    count = slabs * pairs - 1
    return pl.pallas_call(
        functools.partial(exchange_kernel, slabs, pairs, pick),
        out_shape=jax.ShapeDtypeStruct(shape, jnp.float32),
        in_specs=[anywhere],
        out_specs=anywhere,
        scratch_shapes=[
            pltpu.SemaphoreType.DMA,
            pltpu.SemaphoreType.DMA((count,)),
            pltpu.SemaphoreType.DMA((count,)),
        ],
        compiler_params=pltpu.CompilerParams(collective_id=collective_id, has_side_effects=True),
        name=name,
    )(values)


def half_turn(values):
    return pltpu.roll(values, values.shape[1] // 2, 1)


def cross_kernel(rows, total, place, matches, damping, radius, fh, fl, ih, il, src, out, spec, mags):
    maps, depth = len(matches.shape) and matches.shape[0], radius.shape[1]
    lanes = radius.shape[2]
    half = rows // 2
    lane = lax.broadcasted_iota(jnp.int32, (depth, lanes), 1)
    left_half = lane < lanes // 2
    real0, imag0 = lane == 0, lane == lanes // 2
    packed = real0 | imag0
    sign = jnp.where(left_half, 1.0, -1.0)
    first_device = place[0] == 0

    def load(s, r):
        return src[s, pl.ds(r, depth, stride=rows)]

    def turned(values):
        return half_turn(values) * sign

    def along_z(matrix, items):
        stacked = [jnp.concatenate([v, turned(v)], 0) for v in items]
        result = left(matrix, jnp.concatenate(stacked, 1))
        return [result[:, i * lanes : (i + 1) * lanes] for i in range(len(items))]

    def crossed(s, row, fx2):
        own = spec[row, s]
        far = spec[row, matches[s]]
        straight = own * far
        skew = own * half_turn(far)
        value = jnp.where(left_half, straight, skew) + half_turn(
            jnp.where(left_half, -skew, straight)
        )
        power = mags[row, s] * mags[row, matches[s]] + FLOOR_VALUE**2
        return value * (jnp.exp(-damping[s] * (radius[row] + fx2)) * lax.rsqrt(power))

    def keep(row, s, value):
        spec[row, s] = value
        square = value * value
        mags[row, s] = square + half_turn(square)

    def pair_of_rows(j, special):
        k = place[0] * half + j
        fx = k.astype(jnp.float32) / total if not isinstance(k, int) else k / total
        fx2 = fx * fx
        count = 3 if special else 2
        items = []
        for s in range(maps):
            a, b = load(s, j), load(s, j + half)
            total_ab, diff = a + b, a - b
            mixed_a = 0.5 * jnp.where(real0, total_ab, diff)
            mixed_b = 0.5 * half_turn(jnp.where(imag0, total_ab, -diff))
            items += [jnp.where(packed, mixed_a, a), jnp.where(packed, mixed_b, b)]
            if special:
                corner = jnp.where(real0, a, 0.0)
                corner = jnp.where(lane == 1, pltpu.roll(a, 1 + lanes // 2, 1), corner)
                corner = jnp.where(lane == 2, pltpu.roll(b, 2, 1), corner)
                corner = jnp.where(lane == 3, pltpu.roll(b, 3 + lanes // 2, 1), corner)
                items.append(corner)
        for i, value in enumerate(along_z((fh, fl), items)):
            keep(i % count, i // count, value)
        second = jnp.where(first_device, 0.25, fx2) if special else fx2
        items = []
        for s in range(maps):
            items += [crossed(s, 0, fx2), crossed(s, 1, second)]
            if special:
                items.append(crossed(s, 2, 0.0))
        items = along_z((ih, il), items)
        for s in range(maps):
            a, b = items[s * count], items[s * count + 1]
            t = half_turn(b)
            mixed_a = jnp.where(real0, a - t, a + t)
            mixed_b = jnp.where(real0, a + t, t - a)
            if special:
                e = items[s * count + 2]
                corner_a = jnp.where(real0, e, pltpu.roll(e, lanes // 2 - 1, 1))
                corner_b = jnp.where(
                    real0, pltpu.roll(e, lanes - 2, 1), pltpu.roll(e, lanes // 2 - 3, 1)
                )
                mixed_a = jnp.where(first_device, corner_a, mixed_a)
                mixed_b = jnp.where(first_device, corner_b, mixed_b)
            out[s, pl.ds(j, depth, stride=rows)] = jnp.where(packed, mixed_a, a)
            out[s, pl.ds(j + half, depth, stride=rows)] = jnp.where(packed, mixed_b, b)

    pair_of_rows(0, True)

    @pl.loop(1, half)
    def _(j):
        pair_of_rows(j, False)


def crossed_back(values, damping, matches, place, total):
    maps, depth, rows, lanes = values.shape
    vmem, smem = pl.BlockSpec(memory_space=pltpu.VMEM), pl.BlockSpec(memory_space=pltpu.SMEM)
    forward, backward = both_z(depth)
    result = pl.pallas_call(
        functools.partial(cross_kernel, rows, total),
        out_shape=jax.ShapeDtypeStruct((maps, depth * rows, lanes), jnp.float32),
        in_specs=[smem] * 3 + [vmem] * 6,
        out_specs=vmem,
        scratch_shapes=[
            pltpu.VMEM((3, maps, depth, lanes), jnp.float32),
            pltpu.VMEM((3, maps, depth, lanes), jnp.float32),
        ],
        compiler_params=pltpu.CompilerParams(vmem_limit_bytes=LIMIT),
        name="cross",
    )(
        place, matches, damping, radii(depth, lanes), *halves(forward), *halves(backward),
        values.reshape(maps, depth * rows, lanes),
    )
    return result.reshape(maps, depth, rows, lanes)


def finish_kernel(yh, yl, xh, xl, src, out):
    blocks, depth, rows, lanes = src.shape
    for i in range(0, depth, 2):
        first = src[:, i].reshape(blocks * rows, lanes)
        second = src[:, i + 1].reshape(blocks * rows, lanes)
        one, two = planes_transformed(first, second, (yh, yl), (xh, xl))
        out[i] = one
        out[i + 1] = two


def finished(values):
    blocks, depth, rows, lanes = values.shape
    step = 4
    y = halves(inverse_y(lanes))
    x = halves(inverse_x(blocks * rows, blocks))
    whole = [pl.BlockSpec(m.shape, lambda i: (0, 0)) for m in (*y, *x)]
    return pl.pallas_call(
        finish_kernel,
        grid=(depth // step,),
        out_shape=jax.ShapeDtypeStruct((depth, blocks * rows, lanes), jnp.float32),
        in_specs=whole + [pl.BlockSpec((blocks, step, rows, lanes), lambda i: (0, i, 0, 0))],
        out_specs=pl.BlockSpec((step, blocks * rows, lanes), lambda i: (i, 0, 0)),
        compiler_params=pltpu.CompilerParams(vmem_limit_bytes=LIMIT),
        name="finish",
    )(*y, *x, values)


def fused(slabs, pairs, occupancy, classes, conductance, damping, matches):
    _, depth, rows, lanes = occupancy.shape
    maps = damping.shape[0]
    share = rows // (slabs * pairs)
    volume = diffused(occupancy[0], classes[0], conductance, slabs, pairs)

    def outward(src, dst, pair, slab, p, q):
        at = pl.multiple_of((p * slabs + q) * share, share)
        return (
            src.at[:, pl.ds(at, share)],
            dst.at[pair, pl.ds(slab * depth, depth)],
        )

    columns = exchange(
        volume, (maps, depth * slabs, share, lanes), outward, slabs, pairs, 1, "spread"
    )
    place = (lax.axis_index("pair") * slabs + lax.axis_index("slab")).astype(jnp.int32)
    columns = crossed_back(columns, damping, matches, place.reshape(1), rows)

    def inward(src, dst, pair, slab, p, q):
        return src.at[p, pl.ds(q * depth, depth)], dst.at[pair * slabs + slab]

    planes = exchange(
        columns, (slabs * pairs, depth, share, lanes), inward, slabs, pairs, 2, "gather"
    )
    return finished(planes)[None]


def solution(mesh):
    in_specs = (
        P(("groups", "pair"), "slab", None, None),
        P(("groups", "pair"), "slab", None, None),
        P(),
        P("groups"),
        P("groups"),
    )
    out_specs = P(("groups", "pair"), "slab", None, None)
    slabs, pairs = mesh.shape["slab"], mesh.shape["pair"]

    def local(occupancy, classes, conductance, damping, matches):
        maps, depth, rows, lanes = occupancy.shape
        share, rest = divmod(rows, slabs * pairs)
        fits = rest == 0 and share % 16 == 0 and depth % 8 == 0 and lanes == 128
        if fits and maps == 1 and damping.shape[0] == pairs:
            return fused(slabs, pairs, occupancy, classes, conductance, damping, matches)
        return plain(occupancy, classes, conductance, damping, matches)

    return jax.shard_map(local, mesh=mesh, in_specs=in_specs, out_specs=out_specs, check_vma=False)
```

```python
import functools
import math

import jax
import jax.numpy as jnp
import ml_dtypes
import numpy as np
from jax import lax
from jax.experimental import pallas as pl
from jax.experimental.pallas import tpu as pltpu
from jax.sharding import PartitionSpec as P

STEPS = 4
STEP_SIZE = 1.0 / 6.0
FLOOR_VALUE = 0.01
PAD = 8
LIMIT = 58 * 1024 * 1024
MESH = pl.DeviceIdType.MESH


FORMS = {1: "bjxy,jk->bkxy", 2: "bzjy,jk->bzky", 3: "bzxj,jk->bzxk"}


def with_halo(shard, sides, width):
    for axis, dim in sides:
        size, length = (lax.axis_size(axis), shard.shape[dim])
        up = [(i, (i + 1) % size) for i in range(size - 1)]
        down = [(j, i) for i, j in up]
        last = lax.slice_in_dim(shard, length - width, length, axis=dim)
        leading = lax.slice_in_dim(shard, 0, width, axis=dim)
        before = lax.ppermute(last, axis, up)
        after = lax.ppermute(leading, axis, down)
        shard = jnp.concatenate([before, shard, after], axis=dim)
    return shard


def tables(length):
    counter = jnp.arange(length, dtype=jnp.int32)
    product = counter[:, None] * counter[None, :] % length
    angles = product.astype(jnp.float32) * (2.0 * math.pi / length)
    factor = 1.0 / math.sqrt(length)
    return (jnp.cos(angles) * factor, jnp.sin(angles) * factor)


def multiply_along(values, matrix, axis_dim):
    return jnp.einsum(FORMS[axis_dim], values, matrix, precision=lax.Precision.HIGHEST)


def forward_real(values, axis_dim):
    cosine, sine_table = tables(values.shape[axis_dim])
    return (multiply_along(values, cosine, axis_dim), -multiply_along(values, sine_table, axis_dim))


def forward_complex(real_part, imag_part, axis_dim):
    cosine, sine_table = tables(real_part.shape[axis_dim])
    return (
        multiply_along(real_part, cosine, axis_dim)
        + multiply_along(imag_part, sine_table, axis_dim),
        multiply_along(imag_part, cosine, axis_dim)
        - multiply_along(real_part, sine_table, axis_dim),
    )


def inverse_complex(real_part, imag_part, axis_dim):
    cosine, sine_table = tables(real_part.shape[axis_dim])
    return (
        multiply_along(real_part, cosine, axis_dim)
        - multiply_along(imag_part, sine_table, axis_dim),
        multiply_along(imag_part, cosine, axis_dim)
        + multiply_along(real_part, sine_table, axis_dim),
    )


def inverse_real(real_part, imag_part, axis_dim):
    cosine, sine_table = tables(real_part.shape[axis_dim])
    return multiply_along(real_part, cosine, axis_dim) - multiply_along(
        imag_part, sine_table, axis_dim
    )


def local_neighbours(padded):
    widened = jnp.pad(padded, ((0, 0), (0, 0), (1, 1), (1, 1)))
    return [
        widened[:, 2:, 1:-1, 1:-1],
        widened[:, :-2, 1:-1, 1:-1],
        widened[:, 1:-1, 2:, 1:-1],
        widened[:, 1:-1, :-2, 1:-1],
        widened[:, 1:-1, 1:-1, 2:],
        widened[:, 1:-1, 1:-1, :-2],
    ]


def signed_frequency(counter, length):
    return jnp.where(counter < length // 2, counter, counter - length).astype(jnp.float32) / length


def cross_power(own_real, own_imag, far_real, far_imag, decay_rate, offset, whole_rows):
    depth_count = own_real.shape[1]
    row_count = own_real.shape[2]
    width_count = own_real.shape[3]
    along_depth = signed_frequency(jnp.arange(depth_count, dtype=jnp.int32), depth_count)
    along_rows = signed_frequency(offset + jnp.arange(row_count, dtype=jnp.int32), whole_rows)
    along_width = signed_frequency(jnp.arange(width_count, dtype=jnp.int32), width_count)
    radius = (
        along_depth[:, None, None] ** 2
        + along_rows[None, :, None] ** 2
        + along_width[None, None, :] ** 2
    )
    cross_real = own_real * far_real + own_imag * far_imag
    cross_imag = own_imag * far_real - own_real * far_imag
    magnitude = jnp.sqrt((own_real**2 + own_imag**2) * (far_real**2 + far_imag**2) + FLOOR_VALUE**2)
    weight = jnp.exp(-decay_rate[:, None, None, None] * radius[None]) / magnitude
    return (cross_real * weight, cross_imag * weight)


def picked(values, matches):
    return jnp.stack(
        [
            lax.dynamic_index_in_dim(values, matches[i], 0, keepdims=False)
            for i in range(matches.shape[0])
        ]
    )


def spread(values):
    values = lax.all_to_all(values, "pair", split_axis=2, concat_axis=0, tiled=True)
    return lax.all_to_all(values, "slab", split_axis=2, concat_axis=1, tiled=True)


def gathered(values):
    values = lax.all_to_all(values, "slab", split_axis=1, concat_axis=2, tiled=True)
    return lax.all_to_all(values, "pair", split_axis=0, concat_axis=2, tiled=True)


def plain(occupancy, classes, conductance, damping, matches):
    conduct = jnp.zeros(occupancy.shape, jnp.float32)
    for class_id in range(conductance.shape[0]):
        conduct = jnp.where(classes == class_id, conductance[class_id], conduct)
    outer_rims = local_neighbours(with_halo(conduct, (("slab", 1),), 1))
    volume = occupancy
    for sweep_index in range(STEPS):
        beside_all = local_neighbours(with_halo(volume, (("slab", 1),), 1))
        change = jnp.zeros_like(volume)
        for other_field, other_conduct in zip(beside_all, outer_rims):
            change = change + 0.5 * (conduct + other_conduct) * (other_field - volume)
        volume = volume + STEP_SIZE * change
    whole_rows = volume.shape[2]
    real_part, imag_part = forward_real(volume, 3)
    real_part, imag_part = forward_complex(real_part, imag_part, 2)
    real_part, imag_part = (spread(real_part), spread(imag_part))
    real_part, imag_part = forward_complex(real_part, imag_part, 1)
    far_real = picked(real_part, matches)
    far_imag = picked(imag_part, matches)
    offset = (
        lax.axis_index("pair") * lax.axis_size("slab") + lax.axis_index("slab")
    ) * real_part.shape[2]
    cross_real, cross_imag = cross_power(
        real_part, imag_part, far_real, far_imag, damping, offset, whole_rows
    )
    cross_real, cross_imag = inverse_complex(cross_real, cross_imag, 1)
    back_real, back_imag = (gathered(cross_real), gathered(cross_imag))
    back_real, back_imag = inverse_complex(back_real, back_imag, 2)
    return inverse_real(back_real, back_imag, 3)


def halves(matrix):
    high = matrix.astype(np.float32).astype(ml_dtypes.bfloat16)
    low = (matrix - high.astype(np.float64)).astype(ml_dtypes.bfloat16)
    return high, low


def trig(rows, cols, length):
    angle = 2.0 * np.pi * ((np.asarray(rows)[:, None] * np.asarray(cols)[None, :]) % length) / length
    return np.cos(angle) / math.sqrt(length), np.sin(angle) / math.sqrt(length)


def swapped(matrix, axis):
    first, second = np.split(matrix, 2, axis)
    return np.concatenate([second, -first], axis)


def row_order(length, blocks):
    half = length // blocks // 2
    order = []
    for block in range(blocks):
        ahead = [block * half + j for j in range(half)]
        order += ahead + [(length - k) if k else length // 2 for k in ahead]
    return np.array(order)


def forward_y(length):
    half = length // 2
    cosine, sine = trig(np.arange(length), np.arange(half), length)
    imag = -sine
    imag[:, 0] = (1.0 - 2.0 * (np.arange(length) % 2)) / math.sqrt(length)
    table = np.concatenate([cosine, imag], 1)
    return np.concatenate([table, swapped(table, 1)], 1)


def inverse_y(length):
    half = length // 2
    cosine, sine = trig(np.arange(half), np.arange(length), length)
    real, imag = 2.0 * cosine, -2.0 * sine
    real[0] = 1.0 / math.sqrt(length)
    imag[0] = (1.0 - 2.0 * (np.arange(length) % 2)) / math.sqrt(length)
    table = np.concatenate([real, imag], 0)
    other = np.concatenate([-imag, real], 0)
    return np.concatenate([table, other], 1)


def forward_x(length, blocks):
    cosine, sine = trig(row_order(length, blocks), np.arange(length), length)
    return np.concatenate([cosine, sine], 1)


def inverse_x(length, blocks):
    cosine, sine = trig(np.arange(length), row_order(length, blocks), length)
    return np.concatenate([cosine, -sine], 1)


def both_z(length):
    cosine, sine = trig(np.arange(length), np.arange(length), length)
    return np.concatenate([cosine, sine], 1), np.concatenate([cosine, -sine], 1)


def squared(length):
    counter = np.arange(length)
    return (np.where(counter < length // 2, counter, counter - length) / length) ** 2


def radii(depth, width):
    half = width // 2
    lanes = np.arange(width) % half
    along = squared(width)[lanes]
    first = squared(depth)[:, None] + along[None, :]
    other = along.copy()
    other[lanes == 0] = 0.25
    second = squared(depth)[:, None] + other[None, :]
    corner = np.zeros(width)
    corner[lanes == 1], corner[lanes == 2], corner[lanes == 3] = 0.25, 0.25, 0.5
    third = squared(depth)[:, None] + corner[None, :]
    return np.stack([first, second, third]).astype(np.float32)


def split(values):
    high = values.astype(jnp.bfloat16)
    return high, (values - high.astype(jnp.float32)).astype(jnp.bfloat16)


def dot(a, b):
    return jnp.dot(a, b, preferred_element_type=jnp.float32)


def left(matrix, values):
    high, low = split(values)
    return dot(matrix[0][...], high) + (dot(matrix[0][...], low) + dot(matrix[1][...], high))


def right(values, matrix):
    high, low = split(values)
    return dot(high, matrix[0][...]) + (dot(low, matrix[0][...]) + dot(high, matrix[1][...]))


def planes_transformed(first, second, along_y, along_x):
    rows, lanes = first.shape
    mid = right(jnp.concatenate([first, second], 0), along_y)
    mid = jnp.concatenate(
        [
            jnp.concatenate([mid[:rows, :lanes], mid[rows:, :lanes]], 1),
            jnp.concatenate([mid[:rows, lanes:], mid[rows:, lanes:]], 1),
        ],
        0,
    )
    out = left(along_x, mid)
    return out[:, :lanes], out[:, lanes:]


def diffuse_kernel(
    slabs, cond, occ, cls, yh, yl, xh, xl, out, buf_a, buf_b, cx, cy, cy_last, cz, kept, halo, ends, send, recv
):
    depth, rows, lanes = occ.shape
    tile = min(64, rows)
    group = max(g for g in range(1, 6) if (depth - 2) % g == 0)
    me = lax.axis_index("slab")
    has_low, has_high = me > 0, me < slabs - 1
    low, high = lax.max(me - 1, 0), lax.min(me + 1, slabs - 1)

    barrier = pltpu.get_barrier_semaphore()

    @pl.when(has_low)
    def _():
        pl.semaphore_signal(barrier, inc=1, device_id={"slab": low}, device_id_type=MESH)

    @pl.when(has_high)
    def _():
        pl.semaphore_signal(barrier, inc=1, device_id={"slab": high}, device_id_type=MESH)

    inside = pl.ds(PAD, rows)

    def conduct(plane):
        labels = cls[plane]
        value = jnp.full((rows, lanes), cond[0], jnp.float32)
        for k in range(1, cond.shape[0]):
            value = jnp.where(labels == k, cond[k], value)
        return value

    ends[0] = conduct(0)
    ends[1] = conduct(depth - 1)

    pl.semaphore_wait(barrier, lax.min(me, 1) + lax.min(slabs - 1 - me, 1))

    def copies(slot, lowest, highest):
        down = pltpu.make_async_remote_copy(
            lowest, halo.at[slot, 1], send.at[slot, 0], recv.at[slot, 1],
            device_id={"slab": low}, device_id_type=MESH,
        )
        up = pltpu.make_async_remote_copy(
            highest, halo.at[slot, 0], send.at[slot, 1], recv.at[slot, 0],
            device_id={"slab": high}, device_id_type=MESH,
        )
        return down, up

    def begin(pair):
        pl.when(has_low)(lambda: pair[0].start())
        pl.when(has_high)(lambda: pair[1].start())

    def arrived(pair):
        pl.when(has_low)(lambda: pair[1].wait_recv())
        pl.when(has_high)(lambda: pair[0].wait_recv())

    def sent(pair):
        pl.when(has_low)(lambda: pair[0].wait_send())
        pl.when(has_high)(lambda: pair[1].wait_send())

    kappas = copies(STEPS, ends.at[0], ends.at[1])
    begin(kappas)
    fields = copies(0, occ.at[0], occ.at[depth - 1])
    begin(fields)

    for slot in range(STEPS + 1):

        @pl.when(jnp.logical_not(has_low))
        def _():
            halo[slot, 0] = jnp.zeros((rows, lanes), jnp.float32)

        @pl.when(jnp.logical_not(has_high))
        def _():
            halo[slot, 1] = jnp.zeros((rows, lanes), jnp.float32)

    edge = jnp.zeros((PAD, lanes), jnp.float32)

    @pl.loop(0, depth)
    def _(z):
        buf_b[z, inside] = conduct(z)
        buf_a[z, inside] = occ[z]
        for ref in (buf_a, buf_b):
            ref[z, pl.ds(0, PAD)] = edge
            ref[z, pl.ds(PAD + rows, PAD)] = edge

    scale = 0.5 * STEP_SIZE

    @pl.loop(0, depth)
    def _(z):
        cx[z, pl.ds(0, PAD)] = scale * (buf_b[z, pl.ds(0, PAD)] + buf_b[z, pl.ds(1, PAD)])
        for r in range(0, rows, tile):
            here = buf_b[z, pl.ds(PAD + r, tile)]
            x_next = buf_b[z, pl.ds(PAD + r + 1, tile)]
            cx[z, pl.ds(PAD + r, tile)] = scale * (here + x_next)
            lane = lax.broadcasted_iota(jnp.int32, (tile, lanes), 1)
            y_next = pltpu.roll(here, lanes - 1, 1)
            cy[z, pl.ds(r, tile)] = jnp.where(lane == lanes - 1, 0.0, scale * (here + y_next))
            y_last = pltpu.roll(here, 1, 1)
            cy_last[z, pl.ds(r, tile)] = jnp.where(lane == 0, 0.0, scale * (here + y_last))
            rim = (lane == 0) | (lane == lanes - 1)
            kept[z, pl.ds(r, tile)] = 1.0 - jnp.where(rim, scale * here, 0.0)

    @pl.loop(0, depth - 1)
    def _(z):
        cz[z + 1] = scale * (buf_b[z, inside] + buf_b[z + 1, inside])

    arrived(kappas)
    cz[0] = scale * (buf_b[0, inside] + halo[STEPS, 0])
    cz[depth] = scale * (buf_b[depth - 1, inside] + halo[STEPS, 1])

    def update(src, dst, z, r, here, flux_low, flux_high):
        x_next = src[z, pl.ds(PAD + r + 1, tile)]
        x_last = src[z, pl.ds(PAD + r - 1, tile)]
        along_x = cx[z, pl.ds(PAD + r, tile)] * (x_next - here) - cx[
            z, pl.ds(PAD + r - 1, tile)
        ] * (here - x_last)
        along_y = cy[z, pl.ds(r, tile)] * (pltpu.roll(here, lanes - 1, 1) - here) - cy_last[
            z, pl.ds(r, tile)
        ] * (here - pltpu.roll(here, 1, 1))
        dst[z, pl.ds(PAD + r, tile)] = kept[z, pl.ds(r, tile)] * here + (
            along_x + along_y + (flux_high - flux_low)
        )

    bufs = (buf_a, buf_b)
    for step in range(STEPS):
        src, dst = bufs[step % 2], bufs[1 - step % 2]
        arrived(fields)
        sent(fields)
        for r in range(0, rows, tile):
            at, within = pl.ds(PAD + r, tile), pl.ds(r, tile)
            here, after = src[0, at], src[1, at]
            update(
                src, dst, 0, r, here,
                cz[0, within] * (here - halo[step, 0, within]),
                cz[1, within] * (after - here),
            )
            here, before = src[depth - 1, at], src[depth - 2, at]
            update(
                src, dst, depth - 1, r, here,
                cz[depth - 1, within] * (here - before),
                cz[depth, within] * (halo[step, 1, within] - here),
            )
        if step + 1 < STEPS:
            fields = copies(
                step + 1, dst.at[0, inside], dst.at[depth - 1, inside]
            )
            begin(fields)
        for r in range(0, rows, tile):
            at, within = pl.ds(PAD + r, tile), pl.ds(r, tile)

            def body(i, carry):
                here, flux_low = carry
                for z in [1 + i * group + g for g in range(group)]:
                    after = src[z + 1, at]
                    flux_high = cz[z + 1, within] * (after - here)
                    update(src, dst, z, r, here, flux_low, flux_high)
                    here, flux_low = after, flux_high
                return here, flux_low

            first = src[1, at]
            lax.fori_loop(0, (depth - 2) // group, body, (first, cz[1, within] * (first - src[0, at])))
    sent(kappas)

    field = bufs[STEPS % 2]

    @pl.loop(0, depth // 2)
    def _(i):
        one, two = planes_transformed(
            field[2 * i, inside], field[2 * i + 1, inside], (yh, yl), (xh, xl)
        )
        out[2 * i] = one
        out[2 * i + 1] = two


def diffused(occupancy, classes, conductance, slabs, pairs):
    depth, rows, lanes = occupancy.shape
    vmem = pl.BlockSpec(memory_space=pltpu.VMEM)
    y = halves(forward_y(lanes))
    x = halves(forward_x(rows, slabs * pairs))
    padded = (depth, rows + 2 * PAD, lanes)
    return pl.pallas_call(
        functools.partial(diffuse_kernel, slabs),
        out_shape=jax.ShapeDtypeStruct((depth, rows, lanes), jnp.float32),
        in_specs=[pl.BlockSpec(memory_space=pltpu.SMEM)] + [vmem] * 6,
        out_specs=vmem,
        scratch_shapes=[
            pltpu.VMEM(padded, jnp.float32),
            pltpu.VMEM(padded, jnp.float32),
            pltpu.VMEM((depth, rows + PAD, lanes), jnp.float32),
            pltpu.VMEM((depth, rows, lanes), jnp.float32),
            pltpu.VMEM((depth, rows, lanes), jnp.float32),
            pltpu.VMEM((depth + 1, rows, lanes), jnp.float32),
            pltpu.VMEM((depth, rows, lanes), jnp.float32),
            pltpu.VMEM((STEPS + 1, 2, rows, lanes), jnp.float32),
            pltpu.VMEM((2, rows, lanes), jnp.float32),
            pltpu.SemaphoreType.DMA((STEPS + 1, 2)),
            pltpu.SemaphoreType.DMA((STEPS + 1, 2)),
        ],
        compiler_params=pltpu.CompilerParams(
            collective_id=0, has_side_effects=True, vmem_limit_bytes=LIMIT
        ),
        name="diffuse",
    )(conductance, occupancy, classes, *y, *x)


def exchange_kernel(slabs, pairs, pick, src, dst, own_sem, send, recv):
    slab, pair = lax.axis_index("slab"), lax.axis_index("pair")
    shifts = [
        (dp, dq)
        for dq in sorted(range(slabs), key=lambda q: -min(q, slabs - q))
        for dp in range(pairs)
        if (dp, dq) != (0, 0)
    ]
    barrier = pltpu.get_barrier_semaphore()
    peers = [(lax.rem(pair + dp, pairs), lax.rem(slab + dq, slabs)) for dp, dq in shifts]
    for p, q in peers:
        pl.semaphore_signal(barrier, inc=1, device_id={"pair": p, "slab": q}, device_id_type=MESH)
    pl.semaphore_wait(barrier, len(peers))
    copies = []
    for i, (p, q) in enumerate(peers):
        source, target = pick(src, dst, pair, slab, p, q)
        copy = pltpu.make_async_remote_copy(
            source, target, send.at[i], recv.at[i],
            device_id={"pair": p, "slab": q}, device_id_type=MESH,
        )
        copy.start()
        copies.append(copy)
    source, target = pick(src, dst, pair, slab, pair, slab)
    own = pltpu.make_async_copy(source, target, own_sem)
    own.start()
    own.wait()
    for copy in copies:
        copy.wait_recv()
    for copy in copies:
        copy.wait_send()


def exchange(values, shape, pick, slabs, pairs, collective_id, name):
    anywhere = pl.BlockSpec(memory_space=pl.ANY)
    count = slabs * pairs - 1
    return pl.pallas_call(
        functools.partial(exchange_kernel, slabs, pairs, pick),
        out_shape=jax.ShapeDtypeStruct(shape, jnp.float32),
        in_specs=[anywhere],
        out_specs=anywhere,
        scratch_shapes=[
            pltpu.SemaphoreType.DMA,
            pltpu.SemaphoreType.DMA((count,)),
            pltpu.SemaphoreType.DMA((count,)),
        ],
        compiler_params=pltpu.CompilerParams(collective_id=collective_id, has_side_effects=True),
        name=name,
    )(values)


def half_turn(values):
    return pltpu.roll(values, values.shape[1] // 2, 1)


def cross_kernel(rows, total, place, matches, damping, radius, fh, fl, ih, il, src, out, spec, mags):
    maps, depth = len(matches.shape) and matches.shape[0], radius.shape[1]
    lanes = radius.shape[2]
    half = rows // 2
    lane = lax.broadcasted_iota(jnp.int32, (depth, lanes), 1)
    left_half = lane < lanes // 2
    real0, imag0 = lane == 0, lane == lanes // 2
    packed = real0 | imag0
    sign = jnp.where(left_half, 1.0, -1.0)
    first_device = place[0] == 0

    def load(s, r):
        return src[s, pl.ds(r, depth, stride=rows)]

    def turned(values):
        return half_turn(values) * sign

    def along_z(matrix, items):
        stacked = [jnp.concatenate([v, turned(v)], 0) for v in items]
        result = left(matrix, jnp.concatenate(stacked, 1))
        return [result[:, i * lanes : (i + 1) * lanes] for i in range(len(items))]

    def crossed(s, row, fx2):
        own = spec[row, s]
        far = spec[row, matches[s]]
        straight = own * far
        skew = own * half_turn(far)
        value = jnp.where(left_half, straight, skew) + half_turn(
            jnp.where(left_half, -skew, straight)
        )
        power = mags[row, s] * mags[row, matches[s]] + FLOOR_VALUE**2
        return value * (jnp.exp(-damping[s] * (radius[row] + fx2)) * lax.rsqrt(power))

    def keep(row, s, value):
        spec[row, s] = value
        square = value * value
        mags[row, s] = square + half_turn(square)

    def pair_of_rows(j, special):
        k = place[0] * half + j
        fx = k.astype(jnp.float32) / total if not isinstance(k, int) else k / total
        fx2 = fx * fx
        count = 3 if special else 2
        items = []
        for s in range(maps):
            a, b = load(s, j), load(s, j + half)
            total_ab, diff = a + b, a - b
            mixed_a = 0.5 * jnp.where(real0, total_ab, diff)
            mixed_b = 0.5 * half_turn(jnp.where(imag0, total_ab, -diff))
            items += [jnp.where(packed, mixed_a, a), jnp.where(packed, mixed_b, b)]
            if special:
                corner = jnp.where(real0, a, 0.0)
                corner = jnp.where(lane == 1, pltpu.roll(a, 1 + lanes // 2, 1), corner)
                corner = jnp.where(lane == 2, pltpu.roll(b, 2, 1), corner)
                corner = jnp.where(lane == 3, pltpu.roll(b, 3 + lanes // 2, 1), corner)
                items.append(corner)
        for i, value in enumerate(along_z((fh, fl), items)):
            keep(i % count, i // count, value)
        second = jnp.where(first_device, 0.25, fx2) if special else fx2
        items = []
        for s in range(maps):
            items += [crossed(s, 0, fx2), crossed(s, 1, second)]
            if special:
                items.append(crossed(s, 2, 0.0))
        items = along_z((ih, il), items)
        for s in range(maps):
            a, b = items[s * count], items[s * count + 1]
            t = half_turn(b)
            mixed_a = jnp.where(real0, a - t, a + t)
            mixed_b = jnp.where(real0, a + t, t - a)
            if special:
                e = items[s * count + 2]
                corner_a = jnp.where(real0, e, pltpu.roll(e, lanes // 2 - 1, 1))
                corner_b = jnp.where(
                    real0, pltpu.roll(e, lanes - 2, 1), pltpu.roll(e, lanes // 2 - 3, 1)
                )
                mixed_a = jnp.where(first_device, corner_a, mixed_a)
                mixed_b = jnp.where(first_device, corner_b, mixed_b)
            out[s, pl.ds(j, depth, stride=rows)] = jnp.where(packed, mixed_a, a)
            out[s, pl.ds(j + half, depth, stride=rows)] = jnp.where(packed, mixed_b, b)

    pair_of_rows(0, True)

    @pl.loop(1, half)
    def _(j):
        pair_of_rows(j, False)


def crossed_back(values, damping, matches, place, total):
    maps, depth, rows, lanes = values.shape
    vmem, smem = pl.BlockSpec(memory_space=pltpu.VMEM), pl.BlockSpec(memory_space=pltpu.SMEM)
    forward, backward = both_z(depth)
    result = pl.pallas_call(
        functools.partial(cross_kernel, rows, total),
        out_shape=jax.ShapeDtypeStruct((maps, depth * rows, lanes), jnp.float32),
        in_specs=[smem] * 3 + [vmem] * 6,
        out_specs=vmem,
        scratch_shapes=[
            pltpu.VMEM((3, maps, depth, lanes), jnp.float32),
            pltpu.VMEM((3, maps, depth, lanes), jnp.float32),
        ],
        compiler_params=pltpu.CompilerParams(vmem_limit_bytes=LIMIT),
        name="cross",
    )(
        place, matches, damping, radii(depth, lanes), *halves(forward), *halves(backward),
        values.reshape(maps, depth * rows, lanes),
    )
    return result.reshape(maps, depth, rows, lanes)


def finish_kernel(yh, yl, xh, xl, src, out):
    for i in range(0, src.shape[0], 2):
        one, two = planes_transformed(src[i], src[i + 1], (yh, yl), (xh, xl))
        out[i] = one
        out[i + 1] = two


def finished(values, blocks):
    depth, rows, lanes = values.shape
    step = 4
    y = halves(inverse_y(lanes))
    x = halves(inverse_x(rows, blocks))
    whole = [pl.BlockSpec(m.shape, lambda i: (0, 0)) for m in (*y, *x)]
    return pl.pallas_call(
        finish_kernel,
        grid=(depth // step,),
        out_shape=jax.ShapeDtypeStruct((depth, rows, lanes), jnp.float32),
        in_specs=whole + [pl.BlockSpec((step, rows, lanes), lambda i: (i, 0, 0))],
        out_specs=pl.BlockSpec((step, rows, lanes), lambda i: (i, 0, 0)),
        compiler_params=pltpu.CompilerParams(vmem_limit_bytes=LIMIT),
        name="finish",
    )(*y, *x, values)


def fused(slabs, pairs, occupancy, classes, conductance, damping, matches):
    _, depth, rows, lanes = occupancy.shape
    maps = damping.shape[0]
    share = rows // (slabs * pairs)
    volume = diffused(occupancy[0], classes[0], conductance, slabs, pairs)

    def outward(src, dst, pair, slab, p, q):
        at = pl.multiple_of((p * slabs + q) * share, share)
        return (
            src.at[:, pl.ds(at, share)],
            dst.at[pair, pl.ds(slab * depth, depth)],
        )

    columns = exchange(
        volume, (maps, depth * slabs, share, lanes), outward, slabs, pairs, 1, "spread"
    )
    place = (lax.axis_index("pair") * slabs + lax.axis_index("slab")).astype(jnp.int32)
    columns = crossed_back(columns, damping, matches, place.reshape(1), rows)

    def inward(src, dst, pair, slab, p, q):
        return src.at[p, pl.ds(q * depth, depth)], dst.at[
            :, pl.ds(pl.multiple_of((pair * slabs + slab) * share, share), share)
        ]

    planes = exchange(
        columns, (depth, rows, lanes), inward, slabs, pairs, 2, "gather"
    )
    return finished(planes, slabs * pairs)[None]


def solution(mesh):
    in_specs = (
        P(("groups", "pair"), "slab", None, None),
        P(("groups", "pair"), "slab", None, None),
        P(),
        P("groups"),
        P("groups"),
    )
    out_specs = P(("groups", "pair"), "slab", None, None)
    slabs, pairs = mesh.shape["slab"], mesh.shape["pair"]

    def local(occupancy, classes, conductance, damping, matches):
        maps, depth, rows, lanes = occupancy.shape
        share, rest = divmod(rows, slabs * pairs)
        fits = rest == 0 and share % 16 == 0 and depth % 8 == 0 and lanes == 128
        if fits and maps == 1 and damping.shape[0] == pairs:
            return fused(slabs, pairs, occupancy, classes, conductance, damping, matches)
        return plain(occupancy, classes, conductance, damping, matches)

    return jax.shard_map(local, mesh=mesh, in_specs=in_specs, out_specs=out_specs, check_vma=False)
```
